32 devices in a mesh: seq: 4 (over y, core), exp: 8 (over z, x).
Axes of the slice: x: 2, y: 2, z: 4, core: 2. Of those that a mesh axis runs over, the one named last changes fastest.
Arguments:
- frames: bfloat16 [8, 512, 1024], P('exp', 'seq'), may hold values from -6 to 6
- conv_kernel: float32 [31, 1024], replicated, may hold values from -1 to 1
- routes: int32 [8, 512, 2], P('exp', 'seq'), may hold values from 0 to 31, all different within a row; in each aligned block of 128 rows (0 to 127, 128 to 255, ..., all dimensions but the last counted through in order) at most 8 rows name the same one
- gates: float32 [8, 512, 2], P('exp', 'seq'), may hold values from 0.25 to 1
- w_in: bfloat16 [32, 1024, 2048], P('exp', None, 'seq'), may hold values from -0.1875 to 0.1875
- w_out: bfloat16 [32, 2048, 1024], P('exp', 'seq'), may hold values from -0.125 to 0.125
- cotangent: bfloat16 [8, 512, 1024], P('exp', 'seq'), may hold values from -1.5 to 1.5
Outputs:
- mixed: bfloat16 [8, 512, 1024], P('exp', 'seq')
- frames_grad: bfloat16 [8, 512, 1024], P('exp', 'seq')
- w_in_grad: float32 [32, 1024, 2048], P('exp', None, 'seq')
- w_out_grad: float32 [32, 2048, 1024], P('exp', 'seq')
The draws below stay inside these ranges and needn't reach their ends.
Inputs may be any that keep to these rules, and one draw needn't show every extreme that they name: `routes`: each frame names two different experts. Within each aligned block of 128 frames of a recording no expert is named more than 8 times, and in every draw some expert is named exactly 8 times within some block.
All inputs are finite; a program needn't handle non-finite values.
Results may differ from the reference program's by a relative error of at most 0.012.
Values may be sent and summed in bfloat16 or wider, within the bound.
A program may use at most 192 MiB of HBM per device.

```python
import math
import jax
import jax.numpy as jnp
import numpy as np
from jax import lax

D = 1024
HID = 2048
KERNEL = 31
T_DEV = 128
CAP = 8
EXPERTS = 32
LEN = 512
HID_DEV = 512
N_SEQ = 4
N_EXP = 8


def steps_of(own_key, shape, pieces, low, high):
    def one(dim, blocks):
        draws = jax.random.uniform(jax.random.fold_in(jax.random.fold_in(own_key, 6), dim), (blocks,), jnp.float32, low / len(pieces), high / len(pieces))
        return jnp.repeat(jnp.exp(draws), shape[dim] // blocks).reshape((-1,) + (1,) * (len(shape) - dim - 1))

    gain = one(*pieces[0])
    for cut in pieces[1:]:
        gain = gain * one(*cut)
    return gain


def deal_out(stream_key, own, number, rows, amount, top, bound, skew):
    order = jax.random.permutation(stream_key, amount)
    heavy_load, common = shares(amount, rows * top, bound, skew, True), shares(amount, rows * top, bound, skew, False)
    places = jnp.arange(amount)

    def named(lengths, offset_by):
        used = int((lengths > 0).sum())
        fixed = max(1, used // 4)
        passed = fixed + (places - fixed + offset_by * (used - fixed)) % max(1, amount - fixed)
        return jnp.zeros((amount,), jnp.int32).at[order[jnp.where(places < fixed, places, passed)]].set(jnp.asarray(lengths, jnp.int32))

    lengths = jnp.where(number % 4 == 0, named(heavy_load, number // 4), named(common, number - number // 4 - 1))
    mixed = jax.random.permutation(jax.random.fold_in(own, 3), amount)
    donor, taker = mixed[0:amount // 2 * 2:2], mixed[1:amount // 2 * 2:2]
    room = jnp.minimum(lengths[donor] - 1, bound - lengths[taker]) // 2
    room = jnp.where((donor == order[0]) | (taker == order[0]) | (lengths[taker] == 0), 0, jnp.maximum(room, 0))
    passed = jax.random.randint(jax.random.fold_in(own, 4), (amount // 2,), 0, 1 << 20) % (room + 1)
    lengths = lengths.at[donor].add(-passed).at[taker].add(passed)
    members = jnp.searchsorted(jnp.cumsum(lengths), jnp.arange(rows * top), side="right").astype(jnp.int32)
    grid = members.reshape(top, rows).T
    grid = grid[jax.random.permutation(jax.random.fold_in(own, 1), rows)]
    offset_by = jax.random.randint(jax.random.fold_in(own, 2), (rows, 1), 0, top)
    return jnp.take_along_axis(grid, (jnp.arange(top)[None, :] + offset_by) % top, axis=1)


def shares(count, total, reach, skew, full):
    loads = [(1 << 20) // math.isqrt(rank ** skew) + 1 for rank in range(1, count + 1)]
    largest = reach if full else min(reach, max(-(-total // count), total * loads[0] // sum(loads)))
    least = 1 if total - largest >= count - 1 else 0
    counts, spare = [largest] + [least] * (count - 1), total - largest - least * (count - 1)
    while spare > 0:
        candidates = [i for i in range(1, count) if counts[i] < largest] or [i for i in range(1, count) if counts[i] < reach]
        whole, budget = sum([loads[i] for i in candidates]), spare
        for i in candidates:
            addition = min(reach - counts[i], max(1, budget * loads[i] // whole), spare)
            counts[i] = counts[i] + addition
            spare = spare - addition
    return np.array(counts)


def noise(own_key, dims, spread, bound, cuts=(), held_as=jnp.bfloat16):
    array = jax.random.normal(own_key, dims, jnp.float32) * spread
    if len(cuts) > 0:
        array = steps_of(own_key, dims, cuts, -0.22, 0.18) * array
    return jnp.clip(array, min=-bound, max=bound).astype(held_as)


def setup_inputs(seed: int = 0) -> dict:
    arg_keys = jax.random.split(jax.random.key(seed), 8)
    frames = noise(arg_keys[0], (N_EXP, LEN, D), 1.0, 6.0, ((0, 8), (1, 4)))
    conv_kernel = noise(arg_keys[1], (KERNEL, D), KERNEL ** -0.5, 1.0, (), jnp.float32)
    routes_keys = jax.random.split(jax.random.fold_in(arg_keys[2], 1), N_EXP * LEN // T_DEV)
    routes_turns = jax.random.permutation(jax.random.fold_in(arg_keys[2], 3), N_EXP * LEN // T_DEV)
    routes = jax.vmap(lambda own, number: deal_out(jax.random.fold_in(arg_keys[2], 2), own, number, T_DEV, EXPERTS, 2, CAP, 1))(routes_keys, routes_turns).reshape((N_EXP, LEN, 2))
    gates = jnp.clip(0.25 + 0.75 * jax.random.uniform(arg_keys[3], (N_EXP, LEN, 2), jnp.float32) ** steps_of(arg_keys[3], (N_EXP, LEN, 2), ((0, 8), (1, 4)), -0.2, 0.2), 0.25, 1.0)
    w_in = noise(arg_keys[4], (EXPERTS, D, HID), D ** -0.5, 0.1875, ((0, 8), (2, 4)))
    w_out = noise(arg_keys[5], (EXPERTS, HID, D), HID ** -0.5, 0.125, ((0, 8), (1, 4)))
    cotangent = noise(arg_keys[6], (N_EXP, LEN, D), 0.25, 1.5, ((0, 8), (1, 4)))
    return dict(frames=frames, conv_kernel=conv_kernel, routes=routes, gates=gates, w_in=w_in, w_out=w_out, cotangent=cotangent)


def silu_slope(values):
    logistic = jax.nn.sigmoid(values)
    return logistic * (1.0 + values * (1.0 - logistic))


def depthwise(values, kernel, reverse):
    margin = (KERNEL - 1) // 2
    padded = jnp.pad(values, ((0, 0), (margin, margin), (0, 0)))
    length = values.shape[1]
    summed = jnp.zeros_like(values)
    for tap_index in range(KERNEL):
        offset = 2 * margin - tap_index if reverse else tap_index
        summed = summed + kernel[tap_index] * padded[:, offset:offset + length, :]
    return summed


def block_sum(left, right):
    row_total = left.shape[0]
    parts = jnp.einsum("rnh,nhd->nrd", left.reshape(row_total, N_SEQ, HID_DEV).astype(jnp.float32),
                       right.reshape(N_SEQ, HID_DEV, -1).astype(jnp.float32))
    rounded = lax.optimization_barrier(parts.astype(jnp.bfloat16))
    return jnp.sum(rounded.astype(jnp.float32), axis=0).astype(jnp.bfloat16)


def expert_pass(pack):
    up_rows, down_rows, weight_in, weight_out = pack
    pre_act = jnp.dot(up_rows, weight_in, preferred_element_type=jnp.float32)
    activation = jax.nn.silu(pre_act).astype(jnp.bfloat16)
    expert_out = block_sum(activation, weight_out)
    act_grad = jnp.dot(down_rows, weight_out.T, preferred_element_type=jnp.float32)
    pre_grad = (act_grad * silu_slope(pre_act)).astype(jnp.bfloat16)
    input_grad = block_sum(pre_grad, weight_in.T)
    grad_out = jnp.dot(activation.T, down_rows, preferred_element_type=jnp.float32)
    grad_in = jnp.dot(up_rows.T, pre_grad, preferred_element_type=jnp.float32)
    return expert_out, input_grad, grad_in, grad_out


def reference(frames, conv_kernel, routes, gates, w_in, w_out, cotangent):
    mixing = depthwise(frames.astype(jnp.float32), conv_kernel, False)
    hidden = (frames.astype(jnp.float32) + jax.nn.silu(mixing)).astype(jnp.bfloat16)
    blocks = N_EXP * N_SEQ
    expert_ids = routes.reshape(blocks, 2 * T_DEV).astype(jnp.int32)
    onehot = (expert_ids[:, :, None] == jnp.arange(EXPERTS, dtype=jnp.int32)[None, None, :]).astype(jnp.int32)
    slot_rank = jnp.sum((jnp.cumsum(onehot, axis=1) - onehot) * onehot, axis=2).astype(jnp.int32)
    block_index = jnp.broadcast_to(jnp.arange(blocks, dtype=jnp.int32)[:, None], expert_ids.shape)
    up_rows = jnp.repeat(hidden.reshape(blocks, T_DEV, D), 2, axis=1)
    gate_col = gates.reshape(blocks, 2 * T_DEV, 1)
    down_rows = (gate_col * jnp.repeat(cotangent.reshape(blocks, T_DEV, D).astype(jnp.float32), 2, axis=1)).astype(jnp.bfloat16)
    blank_slots = jnp.zeros((EXPERTS, blocks, CAP, D), jnp.bfloat16)
    routed_up = blank_slots.at[expert_ids, block_index, slot_rank].set(up_rows).reshape(EXPERTS, blocks * CAP, D)
    routed_down = blank_slots.at[expert_ids, block_index, slot_rank].set(down_rows).reshape(EXPERTS, blocks * CAP, D)
    expert_outs, expert_grads, w_in_grad, w_out_grad = lax.map(expert_pass, (routed_up, routed_down, w_in, w_out))

    def collect(stacked):
        picked = stacked.reshape(EXPERTS, blocks, CAP, D)[expert_ids, block_index, slot_rank]
        return picked.reshape(N_EXP, LEN, 2, D).astype(jnp.float32)

    mixed = (hidden.astype(jnp.float32) + jnp.sum(gates[..., None] * collect(expert_outs), axis=2)).astype(jnp.bfloat16)
    hidden_grad = cotangent.astype(jnp.float32) + jnp.sum(collect(expert_grads), axis=2)
    conv_back = (hidden_grad * silu_slope(mixing)).astype(jnp.bfloat16)
    frames_grad = (hidden_grad + depthwise(conv_back.astype(jnp.float32), conv_kernel, True)).astype(jnp.bfloat16)
    return (mixed, frames_grad, w_in_grad, w_out_grad)
```

```python
import jax
import jax.numpy as jnp
from jax import lax
from jax.sharding import PartitionSpec as P

KERNEL = 31
CAP = 8
BF16 = jnp.bfloat16
F32 = jnp.float32


def silu_slope(values):
    logistic = jax.nn.sigmoid(values)
    return logistic * (1.0 + values * (1.0 - logistic))


def edge_rows(block):
    width = (KERNEL - 1) // 2
    count = lax.axis_size("seq")
    forward = [(i, i + 1) for i in range(count - 1)]
    backward = [(target, source) for source, target in forward]
    low = lax.ppermute(block[-width:], "seq", forward)
    high = lax.ppermute(block[:width], "seq", backward)
    return jnp.concatenate([low, block, high], axis=0)


def local_conv(padded, kernel, reverse, length):
    margin = (KERNEL - 1) // 2
    summed = jnp.zeros((length, padded.shape[1]), F32)
    for tap_index in range(KERNEL):
        offset = 2 * margin - tap_index if reverse else tap_index
        summed = summed + kernel[tap_index] * padded[offset : offset + length]
    return summed


def per_device(frames, conv_kernel, routes, gates, w_in, w_out, cotangent):
    n_seq = lax.axis_size("seq")
    n_exp = lax.axis_size("exp")
    experts = w_in.shape[0]
    length = frames.shape[1]
    width = frames.shape[2]
    slots = experts * n_exp * CAP
    per_dest = experts * CAP

    ids = routes[0].reshape(2 * length)
    order = jnp.arange(2 * length, dtype=jnp.int32)
    earlier = (ids[:, None] == ids[None, :]) & (order[None, :] < order[:, None])
    places = ids * CAP + jnp.sum(earlier.astype(jnp.int32), axis=1)
    places = places.reshape(length, 2)
    gate_pair = gates[0]
    slot_ids = jnp.arange(slots, dtype=jnp.int32)
    picks = [(places[:, k][:, None] == slot_ids[None, :]) for k in range(2)]
    either = (picks[0] | picks[1]).astype(BF16)
    slot_gate = sum(jnp.sum(jnp.where(picks[k], gate_pair[:, k][:, None], 0.0), axis=0) for k in range(2))

    mixing = local_conv(edge_rows(frames[0]).astype(F32), conv_kernel, False, length)
    hidden = (frames[0].astype(F32) + jax.nn.silu(mixing)).astype(BF16)

    def to_slots(rows):
        return jnp.einsum("ts,td->sd", either, rows, preferred_element_type=F32)

    up = to_slots(hidden).astype(BF16)
    down = (slot_gate[:, None] * to_slots(cotangent[0])).astype(BF16)
    both = jnp.concatenate([up, down], axis=1).reshape(n_exp, per_dest, 2 * width)
    got = lax.all_to_all(both, "exp", split_axis=0, concat_axis=0, tiled=True)
    got = lax.all_gather(got, "seq", axis=0, tiled=False)
    got = got.reshape(n_seq * n_exp, experts, CAP, 2 * width).transpose(1, 0, 2, 3)
    got = got.reshape(experts, n_seq * n_exp * CAP, 2 * width)
    routed_up, routed_down = got[:, :, :width], got[:, :, width:]

    pre_act = jnp.einsum("erd,edh->erh", routed_up, w_in, preferred_element_type=F32)
    activation = jax.nn.silu(pre_act).astype(BF16)
    expert_out = jnp.einsum("erh,ehd->erd", activation, w_out, preferred_element_type=F32).astype(BF16)
    act_grad = jnp.einsum("erd,ehd->erh", routed_down, w_out, preferred_element_type=F32)
    pre_grad = (act_grad * silu_slope(pre_act)).astype(BF16)
    input_grad = jnp.einsum("erh,edh->erd", pre_grad, w_in, preferred_element_type=F32).astype(BF16)
    back = jnp.concatenate([expert_out, input_grad], axis=2)
    back = back.reshape(experts, n_seq, n_exp, CAP, 2 * width).transpose(1, 2, 0, 3, 4)
    back = back.reshape(n_seq, n_exp * per_dest, 2 * width)
    back = lax.psum_scatter(back, "seq", scatter_dimension=0, tiled=False)
    back = back.reshape(n_exp, per_dest, 2 * width)
    back = lax.all_to_all(back, "exp", split_axis=0, concat_axis=0, tiled=True)
    back = back.reshape(slots, 2 * width)

    w_out_grad = jnp.einsum("erh,erd->ehd", activation, routed_down, preferred_element_type=F32)
    w_in_grad = jnp.einsum("erd,erh->edh", routed_up, pre_grad, preferred_element_type=F32)

    mixed = hidden.astype(F32)
    for k in range(2):
        picked = jnp.dot(picks[k].astype(BF16), back[:, :width], preferred_element_type=F32)
        mixed = mixed + gate_pair[:, k][:, None] * picked
    hidden_grad = cotangent[0].astype(F32) + jnp.dot(either, back[:, width:], preferred_element_type=F32)
    conv_back = (hidden_grad * silu_slope(mixing)).astype(BF16)
    spread = local_conv(edge_rows(conv_back).astype(F32), conv_kernel, True, length)
    frames_grad = (hidden_grad + spread).astype(BF16)
    return (mixed.astype(BF16)[None], frames_grad[None], w_in_grad, w_out_grad)


def solution(mesh):
    rows = P("exp", "seq", None)
    in_specs = (rows, P(), rows, rows, P("exp", None, "seq"), rows, rows)
    out_specs = (rows, rows, P("exp", None, "seq"), rows)
    return jax.shard_map(
        per_device, mesh=mesh, in_specs=in_specs, out_specs=out_specs, check_vma=False
    )
```

```python
import functools

import jax
import jax.numpy as jnp
from jax import lax
from jax.experimental import pallas as pl
from jax.experimental.pallas import tpu as pltpu
from jax.sharding import PartitionSpec as P

KERNEL = 31
CAP = 8
BF16 = jnp.bfloat16
F32 = jnp.float32


def silu_slope(values):
    logistic = jax.nn.sigmoid(values)
    return logistic * (1.0 + values * (1.0 - logistic))


def edge_rows(block):
    width = (KERNEL - 1) // 2
    count = lax.axis_size("seq")
    forward = [(i, i + 1) for i in range(count - 1)]
    backward = [(target, source) for source, target in forward]
    low = lax.ppermute(block[-width:], "seq", forward)
    high = lax.ppermute(block[:width], "seq", backward)
    return jnp.concatenate([low, block, high], axis=0)


def local_conv(padded, kernel, reverse, length):
    margin = (KERNEL - 1) // 2
    summed = jnp.zeros((length, padded.shape[1]), F32)
    for tap_index in range(KERNEL):
        offset = 2 * margin - tap_index if reverse else tap_index
        summed = summed + kernel[tap_index] * padded[offset : offset + length]
    return summed


GROUP = 8
MESH = pl.DeviceIdType.MESH
LAST = (((1,), (1,)), ((), ()))


def expert_kernel(
    n_seq, n_exp, send_ref, sort_ref, unsort_ref, w_in_hbm, w_out_hbm,
    back_ref, rows_hbm, act_hbm, pre_hbm,
    held, rows, acts, pres, mate_got, y_got, w_in_ref, w_out_ref,
    exp_send, exp_recv, y_send, y_recv, mate_send, mate_recv,
    back_send, back_recv, y_sum_send, y_sum_recv, pair_send, pair_recv, local_sem,
):
    n_y = n_seq // 2
    experts, row_count, double = rows.shape
    width = double // 2
    block = experts * CAP
    group_rows = GROUP * block
    me_s, me_e = lax.axis_index("seq"), lax.axis_index("exp")
    me_y, me_c = me_s // 2, me_s % 2
    mate = me_y * 2 + 1 - me_c

    def part(s, k):
        return held.at[pl.ds(pl.multiple_of((s * n_exp + k) * block, block), block)]

    def remote(src, dst, send, recv, s, e):
        return pltpu.make_async_remote_copy(
            src_ref=src, dst_ref=dst, send_sem=send, recv_sem=recv,
            device_id=(s, e), device_id_type=MESH,
        )

    def same_core(y):
        return lax.rem(y, n_y) * 2 + me_c

    weights = [
        pltpu.make_async_copy(w_in_hbm, w_in_ref, local_sem.at[0]),
        pltpu.make_async_copy(w_out_hbm, w_out_ref, local_sem.at[1]),
    ]

    barrier = pltpu.get_barrier_semaphore()

    def greet(s, e):
        pl.semaphore_signal(barrier, inc=1, device_id=(s, e), device_id_type=MESH)

    greet(mate, me_e)
    for j in range(1, n_y):
        greet(same_core(me_y + j), me_e)
    for k in range(1, n_exp):
        greet(me_s, lax.rem(me_e + k, n_exp))
    pl.semaphore_wait(barrier, 1 + n_y - 1 + n_exp - 1)

    def exp_copy(k):
        target = lax.rem(me_e + k, n_exp)
        return remote(
            send_ref.at[target], part(me_s, k), exp_send.at[k], exp_recv.at[k], me_s, target
        )

    def y_copy(j, k):
        spot = part(me_s, k)
        return remote(
            spot, spot, y_send.at[j, k], y_recv.at[j, k], same_core(me_y + j), me_e
        )

    def mate_copy(j, k):
        spot = part(same_core(me_y + n_y - j), k)
        return remote(spot, spot, mate_send.at[j, k], mate_recv.at[j, k], mate, me_e)

    def loop(low, high, body):
        def step(k, carry):
            body(k)
            return carry

        lax.fori_loop(low, high, step, 0)

    loop(1, n_exp, lambda k: exp_copy(k).start())
    part(me_s, 0)[...] = send_ref[me_e]

    def pass_on(k):
        for j in range(1, n_y):
            y_copy(j, k).start()
        mate_copy(0, k).start()

    def pass_far(k):
        for j in range(1, n_y):
            y_copy(j, k).wait_recv()
            mate_copy(j, k).start()

    pass_on(0)
    for copy in weights:
        copy.start()

    def arrive(k):
        exp_copy(k).wait_recv()
        pass_on(k)

        @pl.when(k >= 2)
        def _():
            pass_far(k - 2)

    loop(1, n_exp, arrive)
    pass_far(n_exp - 2)
    pass_far(n_exp - 1)

    def settle(k):
        for j in range(n_y):
            mate_copy(j, k).wait()
        for j in range(1, n_y):
            y_copy(j, k).wait_send()

    loop(0, n_exp, settle)
    loop(1, n_exp, lambda k: exp_copy(k).wait_send())

    small = group_rows // experts
    columns = 512

    def sort(g):
        span = pl.ds(pl.multiple_of(g * group_rows, group_rows), group_rows)
        out_span = pl.ds(pl.multiple_of(g * small, small), small)
        for col in range(0, double, columns):
            cols = slice(col, col + columns)
            placed = jnp.dot(
                sort_ref[...], held[span, cols], preferred_element_type=F32
            ).astype(BF16)
            for n in range(experts):
                rows[n, out_span, cols] = placed[n * small : (n + 1) * small]

    groups = n_seq * n_exp // GROUP
    loop(0, groups, sort)
    rows_copy = pltpu.make_async_copy(rows, rows_hbm, local_sem.at[2])
    rows_copy.start()
    for copy in weights:
        copy.wait()

    tile = 256
    tiles = row_count // tile

    def hidden_units(i):
        n, span = i // tiles, pl.ds(pl.multiple_of((i % tiles) * tile, tile), tile)
        pre_act = jnp.dot(rows[n, span, :width], w_in_ref[n], preferred_element_type=F32)
        act_grad = lax.dot_general(
            rows[n, span, width:], w_out_ref[n], LAST, preferred_element_type=F32
        )
        logistic = jax.nn.sigmoid(pre_act)
        acts[n, span, :] = (pre_act * logistic).astype(BF16)
        pres[n, span, :] = (
            act_grad * (logistic * (1.0 + pre_act * (1.0 - logistic)))
        ).astype(BF16)

    loop(0, experts * tiles, hidden_units)
    act_copy = pltpu.make_async_copy(acts, act_hbm, local_sem.at[3])
    pre_copy = pltpu.make_async_copy(pres, pre_hbm, local_sem.at[4])
    act_copy.start()
    pre_copy.start()
    rows_copy.wait()

    def partials(i):
        n, span = i // tiles, pl.ds(pl.multiple_of((i % tiles) * tile, tile), tile)
        rows[n, span, :width] = jnp.dot(
            acts[n, span, :], w_out_ref[n], preferred_element_type=F32
        ).astype(BF16)
        rows[n, span, width:] = lax.dot_general(
            pres[n, span, :], w_in_ref[n], LAST, preferred_element_type=F32
        ).astype(BF16)

    loop(0, experts * tiles, partials)

    def unsort(g):
        span = pl.ds(pl.multiple_of(g * group_rows, group_rows), group_rows)
        in_span = pl.ds(pl.multiple_of(g * small, small), small)
        for col in range(0, double, columns):
            cols = slice(col, col + columns)
            stacked = jnp.concatenate([rows[n, in_span, cols] for n in range(experts)], axis=0)
            held[span, cols] = jnp.dot(
                unsort_ref[...], stacked, preferred_element_type=F32
            ).astype(BF16)

    loop(0, groups, unsort)

    def pair_copy(j, k):
        y = lax.rem(me_y + j, n_y)
        return remote(
            part(y * 2 + 1 - me_c, k), mate_got.at[y, k],
            pair_send.at[j, k], pair_recv.at[j, k], mate, me_e,
        )

    def y_sum_copy(j, k):
        target = same_core(me_y + j)
        return remote(
            part(target, k), y_got.at[j - 1, k],
            y_sum_send.at[j, k], y_sum_recv.at[j, k], target, me_e,
        )

    def home_copy(k):
        return remote(
            part(me_s, k), back_ref.at[me_e], back_send.at[k], back_recv.at[k],
            me_s, lax.rem(me_e + n_exp - k, n_exp),
        )

    def order(i):
        return lax.rem(i + 1, n_exp)

    def pair_start(i):
        for j in [*range(1, n_y), 0]:
            pair_copy(j, order(i)).start()

    def y_stage(i):
        k = order(i)
        for j in range(1, n_y):
            pair_copy(j, k).wait_recv()
            y = lax.rem(me_y + j, n_y)
            spot = part(y * 2 + me_c, k)
            spot[...] = (spot[...].astype(F32) + mate_got[y, k].astype(F32)).astype(BF16)
            y_sum_copy(j, k).start()

    def total(k):
        pair_copy(0, k).wait_recv()
        summed = part(me_s, k)[...].astype(F32) + mate_got[me_y, k].astype(F32)
        for j in range(1, n_y):
            y_sum_copy(j, k).wait_recv()
            summed = summed + y_got[j - 1, k].astype(F32)
        return summed.astype(BF16)

    loop(0, n_exp, pair_start)
    loop(0, n_exp, y_stage)

    def home_stage(k):
        part(me_s, k)[...] = total(k)
        home_copy(k).start()

    loop(1, n_exp, home_stage)
    back_ref[me_e] = total(0)

    def finish(k):
        for j in range(n_y):
            pair_copy(j, k).wait_send()
        for j in range(1, n_y):
            y_sum_copy(j, k).wait_send()

    loop(0, n_exp, finish)

    def come_home(k):
        home_copy(k).wait_send()
        pltpu.make_async_remote_copy(
            src_ref=part(me_s, k), dst_ref=back_ref.at[lax.rem(me_e + k, n_exp)],
            send_sem=back_send.at[k], recv_sem=back_recv.at[k],
            device_id=(me_s, lax.rem(me_e + n_exp - k, n_exp)), device_id_type=MESH,
        ).wait_recv()

    loop(1, n_exp, come_home)
    act_copy.wait()
    pre_copy.wait()


def run_experts(both, w_in, w_out):
    n_seq, n_exp = lax.axis_size("seq"), lax.axis_size("exp")
    experts, width, units = w_in.shape
    block = experts * CAP
    row_count = n_seq * n_exp * CAP
    span = GROUP * block
    spot = jnp.arange(span, dtype=jnp.int32)
    expert, rest = spot // (GROUP * CAP), spot % (GROUP * CAP)
    source = (rest // CAP) * block + expert * CAP + rest % CAP
    sort = (source[:, None] == spot[None, :]).astype(BF16)
    n_y = n_seq // 2
    vmem, hbm = pl.BlockSpec(memory_space=pltpu.VMEM), pl.BlockSpec(memory_space=pl.ANY)
    flat, pairs = pltpu.SemaphoreType.DMA((n_exp,)), pltpu.SemaphoreType.DMA((n_y, n_exp))
    return pl.pallas_call(
        functools.partial(expert_kernel, n_seq, n_exp),
        out_shape=(
            jax.ShapeDtypeStruct((n_exp, block, 2 * width), BF16),
            jax.ShapeDtypeStruct((experts, row_count, 2 * width), BF16),
            jax.ShapeDtypeStruct((experts, row_count, units), BF16),
            jax.ShapeDtypeStruct((experts, row_count, units), BF16),
        ),
        in_specs=[vmem, vmem, vmem, hbm, hbm],
        out_specs=(vmem, hbm, hbm, hbm),
        scratch_shapes=[
            pltpu.VMEM((n_seq * n_exp * block, 2 * width), BF16),
            pltpu.VMEM((experts, row_count, 2 * width), BF16),
            pltpu.VMEM((experts, row_count, units), BF16),
            pltpu.VMEM((experts, row_count, units), BF16),
            pltpu.VMEM((n_y, n_exp, block, 2 * width), BF16),
            pltpu.VMEM((n_y - 1, n_exp, block, 2 * width), BF16),
            pltpu.VMEM(w_in.shape, BF16),
            pltpu.VMEM(w_out.shape, BF16),
            flat, flat, pairs, pairs, pairs, pairs,
            flat, flat, pairs, pairs, pairs, pairs,
            pltpu.SemaphoreType.DMA((5,)),
        ],
        compiler_params=pltpu.CompilerParams(
            collective_id=0, has_side_effects=True, vmem_limit_bytes=63 * 1024 * 1024
        ),
        name="expert_exchange",
    )(both, sort, sort.T, w_in, w_out)


def per_device(frames, conv_kernel, routes, gates, w_in, w_out, cotangent):
    n_seq = lax.axis_size("seq")
    n_exp = lax.axis_size("exp")
    experts = w_in.shape[0]
    length = frames.shape[1]
    width = frames.shape[2]
    slots = experts * n_exp * CAP
    per_dest = experts * CAP

    ids = routes[0].reshape(2 * length)
    order = jnp.arange(2 * length, dtype=jnp.int32)
    earlier = (ids[:, None] == ids[None, :]) & (order[None, :] < order[:, None])
    places = ids * CAP + jnp.sum(earlier.astype(jnp.int32), axis=1)
    places = places.reshape(length, 2)
    gate_pair = gates[0]
    slot_ids = jnp.arange(slots, dtype=jnp.int32)
    picks = [(places[:, k][:, None] == slot_ids[None, :]) for k in range(2)]
    either = (picks[0] | picks[1]).astype(BF16)
    slot_gate = sum(jnp.sum(jnp.where(picks[k], gate_pair[:, k][:, None], 0.0), axis=0) for k in range(2))

    mixing = local_conv(edge_rows(frames[0]).astype(F32), conv_kernel, False, length)
    hidden = (frames[0].astype(F32) + jax.nn.silu(mixing)).astype(BF16)

    def to_slots(rows):
        return jnp.einsum("ts,td->sd", either, rows, preferred_element_type=F32)

    up = to_slots(hidden).astype(BF16)
    down = (slot_gate[:, None] * to_slots(cotangent[0])).astype(BF16)
    both = jnp.concatenate([up, down], axis=1).reshape(n_exp, per_dest, 2 * width)
    back, routed, activation, pre_grad = run_experts(both, w_in, w_out)
    routed_up, routed_down = routed[:, :, :width], routed[:, :, width:]
    back = back.reshape(slots, 2 * width)

    w_out_grad = jnp.einsum("erh,erd->ehd", activation, routed_down, preferred_element_type=F32)
    w_in_grad = jnp.einsum("erd,erh->edh", routed_up, pre_grad, preferred_element_type=F32)

    mixed = hidden.astype(F32)
    for k in range(2):
        picked = jnp.dot(picks[k].astype(BF16), back[:, :width], preferred_element_type=F32)
        mixed = mixed + gate_pair[:, k][:, None] * picked
    hidden_grad = cotangent[0].astype(F32) + jnp.dot(either, back[:, width:], preferred_element_type=F32)
    conv_back = (hidden_grad * silu_slope(mixing)).astype(BF16)
    spread = local_conv(edge_rows(conv_back).astype(F32), conv_kernel, True, length)
    frames_grad = (hidden_grad + spread).astype(BF16)
    return (mixed.astype(BF16)[None], frames_grad[None], w_in_grad, w_out_grad)


def solution(mesh):
    rows = P("exp", "seq", None)
    in_specs = (rows, P(), rows, rows, P("exp", None, "seq"), rows, rows)
    out_specs = (rows, rows, P("exp", None, "seq"), rows)
    return jax.shard_map(
        per_device, mesh=mesh, in_specs=in_specs, out_specs=out_specs, check_vma=False
    )
```

```python
import functools

import jax
import jax.numpy as jnp
from jax import lax
from jax.experimental import pallas as pl
from jax.experimental.pallas import tpu as pltpu
from jax.sharding import PartitionSpec as P

KERNEL = 31
CAP = 8
BF16 = jnp.bfloat16
F32 = jnp.float32


def silu_slope(values):
    logistic = jax.nn.sigmoid(values)
    return logistic * (1.0 + values * (1.0 - logistic))


def edge_rows(block):
    width = (KERNEL - 1) // 2
    count = lax.axis_size("seq")
    forward = [(i, i + 1) for i in range(count - 1)]
    backward = [(target, source) for source, target in forward]
    low = lax.ppermute(block[-width:], "seq", forward)
    high = lax.ppermute(block[:width], "seq", backward)
    return jnp.concatenate([low, block, high], axis=0)


def local_conv(padded, kernel, reverse, length):
    margin = (KERNEL - 1) // 2
    summed = jnp.zeros((length, padded.shape[1]), F32)
    for tap_index in range(KERNEL):
        offset = 2 * margin - tap_index if reverse else tap_index
        summed = summed + kernel[tap_index] * padded[offset : offset + length]
    return summed


GROUP = 8
MESH = pl.DeviceIdType.MESH
LAST = (((1,), (1,)), ((), ()))


def expert_kernel(
    n_seq, n_exp, send_ref, sort_ref, unsort_ref, w_in_hbm, w_out_hbm,
    back_ref, rows_hbm, act_hbm, pre_hbm,
    held, rows, acts, pres, mate_got, y_got, w_in_ref, w_out_ref,
    exp_send, exp_recv, y_send, y_recv, mate_send, mate_recv,
    back_send, back_recv, y_sum_send, y_sum_recv, pair_send, pair_recv, local_sem,
):
    n_y = n_seq // 2
    experts, row_count, double = rows.shape
    width = double // 2
    block = experts * CAP
    group_rows = GROUP * block
    me_s, me_e = lax.axis_index("seq"), lax.axis_index("exp")
    me_y, me_c = me_s // 2, me_s % 2
    mate = me_y * 2 + 1 - me_c

    def part(s, k):
        return held.at[pl.ds(pl.multiple_of((s * n_exp + k) * block, block), block)]

    def remote(src, dst, send, recv, s, e):
        return pltpu.make_async_remote_copy(
            src_ref=src, dst_ref=dst, send_sem=send, recv_sem=recv,
            device_id=(s, e), device_id_type=MESH,
        )

    def other(k):
        total, bit = 0, 1
        while bit < n_exp:
            total = total + lax.rem(me_e // bit + k // bit, 2) * bit
            bit *= 2
        return total

    def same_core(y):
        return lax.rem(y, n_y) * 2 + me_c

    weights = [
        pltpu.make_async_copy(w_in_hbm, w_in_ref, local_sem.at[0]),
        pltpu.make_async_copy(w_out_hbm, w_out_ref, local_sem.at[1]),
    ]

    barrier = pltpu.get_barrier_semaphore()

    def greet(s, e):
        pl.semaphore_signal(barrier, inc=1, device_id=(s, e), device_id_type=MESH)

    greet(mate, me_e)
    for j in range(1, n_y):
        greet(same_core(me_y + j), me_e)
    for k in range(1, n_exp):
        greet(me_s, other(k))
    pl.semaphore_wait(barrier, 1 + n_y - 1 + n_exp - 1)

    def exp_copy(k):
        target = other(k)
        return remote(
            send_ref.at[target], part(me_s, k), exp_send.at[k], exp_recv.at[k], me_s, target
        )

    def y_copy(j, k):
        spot = part(me_s, k)
        return remote(
            spot, spot, y_send.at[j, k], y_recv.at[j, k], same_core(me_y + j), me_e
        )

    def mate_copy(j, k):
        spot = part(same_core(me_y + n_y - j), k)
        return remote(spot, spot, mate_send.at[j, k], mate_recv.at[j, k], mate, me_e)

    def loop(low, high, body):
        def step(k, carry):
            body(k)
            return carry

        lax.fori_loop(low, high, step, 0)

    half = n_exp // 2
    for k in [1, half, half + 1, *range(2, half)]:
        exp_copy(k).start()
    part(me_s, 0)[...] = send_ref[me_e]

    def pass_on(k):
        for j in range(1, n_y):
            y_copy(j, k).start()
        mate_copy(0, k).start()

    def pass_far(k):
        for j in range(1, n_y):
            y_copy(j, k).wait_recv()
            mate_copy(j, k).start()

    pass_on(0)
    for copy in weights:
        copy.start()

    def arrive(k):
        exp_copy(k).wait_recv()
        pass_on(k)

        @pl.when((k >= half) & (k < n_exp - 2))
        def _():
            exp_copy(k).wait_send()
            exp_copy(k + 2).start()

        @pl.when(k >= half)
        def _():
            pass_far(k - half)

    loop(1, n_exp, arrive)
    loop(half, n_exp, pass_far)

    def settle(k):
        for j in range(n_y):
            mate_copy(j, k).wait()
        for j in range(1, n_y):
            y_copy(j, k).wait_send()

    loop(0, n_exp, settle)
    for k in [*range(1, half), n_exp - 2, n_exp - 1]:
        exp_copy(k).wait_send()

    small = group_rows // experts
    columns = 512

    def sort(g):
        span = pl.ds(pl.multiple_of(g * group_rows, group_rows), group_rows)
        out_span = pl.ds(pl.multiple_of(g * small, small), small)
        for col in range(0, double, columns):
            cols = slice(col, col + columns)
            placed = jnp.dot(
                sort_ref[...], held[span, cols], preferred_element_type=F32
            ).astype(BF16)
            for n in range(experts):
                rows[n, out_span, cols] = placed[n * small : (n + 1) * small]

    groups = n_seq * n_exp // GROUP
    loop(0, groups, sort)
    rows_copy = pltpu.make_async_copy(rows, rows_hbm, local_sem.at[2])
    rows_copy.start()
    for copy in weights:
        copy.wait()

    tile = 256
    tiles = row_count // tile

    def hidden_units(i):
        n, span = i // tiles, pl.ds(pl.multiple_of((i % tiles) * tile, tile), tile)
        pre_act = jnp.dot(rows[n, span, :width], w_in_ref[n], preferred_element_type=F32)
        act_grad = lax.dot_general(
            rows[n, span, width:], w_out_ref[n], LAST, preferred_element_type=F32
        )
        logistic = jax.nn.sigmoid(pre_act)
        acts[n, span, :] = (pre_act * logistic).astype(BF16)
        pres[n, span, :] = (
            act_grad * (logistic * (1.0 + pre_act * (1.0 - logistic)))
        ).astype(BF16)

    loop(0, experts * tiles, hidden_units)
    act_copy = pltpu.make_async_copy(acts, act_hbm, local_sem.at[3])
    pre_copy = pltpu.make_async_copy(pres, pre_hbm, local_sem.at[4])
    act_copy.start()
    pre_copy.start()
    rows_copy.wait()

    def partials(i):
        n, span = i // tiles, pl.ds(pl.multiple_of((i % tiles) * tile, tile), tile)
        rows[n, span, :width] = jnp.dot(
            acts[n, span, :], w_out_ref[n], preferred_element_type=F32
        ).astype(BF16)
        rows[n, span, width:] = lax.dot_general(
            pres[n, span, :], w_in_ref[n], LAST, preferred_element_type=F32
        ).astype(BF16)

    loop(0, experts * tiles, partials)

    def unsort(g):
        span = pl.ds(pl.multiple_of(g * group_rows, group_rows), group_rows)
        in_span = pl.ds(pl.multiple_of(g * small, small), small)
        for col in range(0, double, columns):
            cols = slice(col, col + columns)
            stacked = jnp.concatenate([rows[n, in_span, cols] for n in range(experts)], axis=0)
            held[span, cols] = jnp.dot(
                unsort_ref[...], stacked, preferred_element_type=F32
            ).astype(BF16)

    loop(0, groups, unsort)

    def pair_copy(j, k):
        y = lax.rem(me_y + j, n_y)
        return remote(
            part(y * 2 + 1 - me_c, k), mate_got.at[y, k],
            pair_send.at[j, k], pair_recv.at[j, k], mate, me_e,
        )

    def y_sum_copy(j, k):
        target = same_core(me_y + j)
        return remote(
            part(target, k), y_got.at[j - 1, k],
            y_sum_send.at[j, k], y_sum_recv.at[j, k], target, me_e,
        )

    def home_copy(k):
        return remote(
            part(me_s, k), back_ref.at[me_e], back_send.at[k], back_recv.at[k],
            me_s, other(k),
        )

    def y_stage(k):
        for j in range(1, n_y):
            pair_copy(j, k).wait_recv()
            y = lax.rem(me_y + j, n_y)
            spot = part(y * 2 + me_c, k)
            spot[...] = (spot[...].astype(F32) + mate_got[y, k].astype(F32)).astype(BF16)
            y_sum_copy(j, k).start()

    def total(k):
        pair_copy(0, k).wait_recv()
        summed = part(me_s, k)[...].astype(F32) + mate_got[me_y, k].astype(F32)
        for j in range(1, n_y):
            y_sum_copy(j, k).wait_recv()
            summed = summed + y_got[j - 1, k].astype(F32)
        return summed.astype(BF16)

    def home_stage(k):
        if k == 0:
            back_ref[me_e] = total(0)
        else:
            part(me_s, k)[...] = total(k)
            home_copy(k).start()

    def y_sent(k):
        for j in range(1, n_y):
            y_sum_copy(j, k).wait_send()

    order = [*range(half, n_exp), *range(1, half), 0]
    for k in order:
        for j in range(1, n_y):
            pair_copy(j, k).start()
    for k in order:
        pair_copy(0, k).start()
    for i, k in enumerate(order):
        if i >= 2:
            y_sent(order[i - 2])
        y_stage(k)
        if i >= 2:
            home_stage(order[i - 2])
    for k in order[-2:]:
        home_stage(k)
        y_sent(k)

    def finish(k):
        for j in range(n_y):
            pair_copy(j, k).wait_send()

    loop(0, n_exp, finish)

    def come_home(k):
        home_copy(k).wait_send()
        remote(
            part(me_s, k), back_ref.at[other(k)], back_send.at[k], back_recv.at[k],
            me_s, other(k),
        ).wait_recv()

    loop(1, n_exp, come_home)
    act_copy.wait()
    pre_copy.wait()


def run_experts(both, w_in, w_out):
    n_seq, n_exp = lax.axis_size("seq"), lax.axis_size("exp")
    experts, width, units = w_in.shape
    block = experts * CAP
    row_count = n_seq * n_exp * CAP
    span = GROUP * block
    spot = jnp.arange(span, dtype=jnp.int32)
    expert, rest = spot // (GROUP * CAP), spot % (GROUP * CAP)
    source = (rest // CAP) * block + expert * CAP + rest % CAP
    sort = (source[:, None] == spot[None, :]).astype(BF16)
    n_y = n_seq // 2
    vmem, hbm = pl.BlockSpec(memory_space=pltpu.VMEM), pl.BlockSpec(memory_space=pl.ANY)
    flat, pairs = pltpu.SemaphoreType.DMA((n_exp,)), pltpu.SemaphoreType.DMA((n_y, n_exp))
    return pl.pallas_call(
        functools.partial(expert_kernel, n_seq, n_exp),
        out_shape=(
            jax.ShapeDtypeStruct((n_exp, block, 2 * width), BF16),
            jax.ShapeDtypeStruct((experts, row_count, 2 * width), BF16),
            jax.ShapeDtypeStruct((experts, row_count, units), BF16),
            jax.ShapeDtypeStruct((experts, row_count, units), BF16),
        ),
        in_specs=[vmem, vmem, vmem, hbm, hbm],
        out_specs=(vmem, hbm, hbm, hbm),
        scratch_shapes=[
            pltpu.VMEM((n_seq * n_exp * block, 2 * width), BF16),
            pltpu.VMEM((experts, row_count, 2 * width), BF16),
            pltpu.VMEM((experts, row_count, units), BF16),
            pltpu.VMEM((experts, row_count, units), BF16),
            pltpu.VMEM((n_y, n_exp, block, 2 * width), BF16),
            pltpu.VMEM((n_y - 1, n_exp, block, 2 * width), BF16),
            pltpu.VMEM(w_in.shape, BF16),
            pltpu.VMEM(w_out.shape, BF16),
            flat, flat, pairs, pairs, pairs, pairs,
            flat, flat, pairs, pairs, pairs, pairs,
            pltpu.SemaphoreType.DMA((5,)),
        ],
        compiler_params=pltpu.CompilerParams(
            collective_id=0, has_side_effects=True, vmem_limit_bytes=63 * 1024 * 1024
        ),
        name="expert_exchange",
    )(both, sort, sort.T, w_in, w_out)


def per_device(frames, conv_kernel, routes, gates, w_in, w_out, cotangent):
    n_seq = lax.axis_size("seq")
    n_exp = lax.axis_size("exp")
    experts = w_in.shape[0]
    length = frames.shape[1]
    width = frames.shape[2]
    slots = experts * n_exp * CAP
    per_dest = experts * CAP

    ids = routes[0].reshape(2 * length)
    order = jnp.arange(2 * length, dtype=jnp.int32)
    earlier = (ids[:, None] == ids[None, :]) & (order[None, :] < order[:, None])
    places = ids * CAP + jnp.sum(earlier.astype(jnp.int32), axis=1)
    places = places.reshape(length, 2)
    gate_pair = gates[0]
    slot_ids = jnp.arange(slots, dtype=jnp.int32)
    picks = [(places[:, k][:, None] == slot_ids[None, :]) for k in range(2)]
    either = (picks[0] | picks[1]).astype(BF16)
    slot_gate = sum(jnp.sum(jnp.where(picks[k], gate_pair[:, k][:, None], 0.0), axis=0) for k in range(2))

    mixing = local_conv(edge_rows(frames[0]).astype(F32), conv_kernel, False, length)
    hidden = (frames[0].astype(F32) + jax.nn.silu(mixing)).astype(BF16)

    def to_slots(rows):
        return jnp.einsum("ts,td->sd", either, rows, preferred_element_type=F32)

    up = to_slots(hidden).astype(BF16)
    down = (slot_gate[:, None] * to_slots(cotangent[0])).astype(BF16)
    both = jnp.concatenate([up, down], axis=1).reshape(n_exp, per_dest, 2 * width)
    back, routed, activation, pre_grad = run_experts(both, w_in, w_out)
    routed_up, routed_down = routed[:, :, :width], routed[:, :, width:]
    back = back.reshape(slots, 2 * width)

    w_out_grad = jnp.einsum("erh,erd->ehd", activation, routed_down, preferred_element_type=F32)
    w_in_grad = jnp.einsum("erd,erh->edh", routed_up, pre_grad, preferred_element_type=F32)

    mixed = hidden.astype(F32)
    for k in range(2):
        picked = jnp.dot(picks[k].astype(BF16), back[:, :width], preferred_element_type=F32)
        mixed = mixed + gate_pair[:, k][:, None] * picked
    hidden_grad = cotangent[0].astype(F32) + jnp.dot(either, back[:, width:], preferred_element_type=F32)
    conv_back = (hidden_grad * silu_slope(mixing)).astype(BF16)
    spread = local_conv(edge_rows(conv_back).astype(F32), conv_kernel, True, length)
    frames_grad = (hidden_grad + spread).astype(BF16)
    return (mixed.astype(BF16)[None], frames_grad[None], w_in_grad, w_out_grad)


def solution(mesh):
    rows = P("exp", "seq", None)
    in_specs = (rows, P(), rows, rows, P("exp", None, "seq"), rows, rows)
    out_specs = (rows, rows, P("exp", None, "seq"), rows)
    return jax.shard_map(
        per_device, mesh=mesh, in_specs=in_specs, out_specs=out_specs, check_vma=False
    )
```
